128 devices in a mesh: row: 8 (over z, x_lo), col: 16 (over y, x_hi, core).
Axes of the slice: x: 4 (x_hi: 2, x_lo: 2; x = x_hi * 2 + x_lo), y: 4, z: 4, core: 2. Of those that a mesh axis runs over, the one named last changes fastest.
Arguments:
- left_factor: float32 [20480, 2048], P('row', 'col'), may hold values from -0.125 to 0.125
- right_factor: float32 [2048, 20480], P('row', 'col'), may hold values from -6 to 6
- pair_gap: float32 [2048], P('col'), may hold values from 0.05 to 2
- mask_left: int32 [160, 16], P('row', 'col'), may hold values 0 or 1
- mask_right: int32 [16, 160], P('row', 'col'), may hold values 0 or 1
Outputs:
- update: float32 [20480, 20480], P('row', 'col')
The draws below stay inside these ranges and needn't reach their ends.
All inputs are finite; a program needn't handle non-finite values. No bound on the sum of `mask_left` or of `mask_right` on one device may be relied on, other than what follows from the above.
Results may differ from the reference program's by a relative error of at most 0.00008.
Values sent between devices are 32-bit elements; how exact they have to be, the bound alone decides.
A program may use at most 128 MiB of HBM per device.

```python
import math
import jax
import jax.numpy as jnp
from jax import lax

NAUX = 20480
BLK = 128
PAIRS = 2048


def with_ends(result, rng, smallest, top_value):
    extent = result.shape
    index_at = [jax.random.randint(jax.random.fold_in(rng, axis), (), 0, extent[axis]) for axis in range(len(extent))]
    result = result.at[tuple(index_at)].set(smallest)
    longest = extent.index(max(extent))
    index_at[longest] = (index_at[longest] + 1) % extent[longest]
    return result.at[tuple(index_at)].set(top_value)


def steps_of(key, dims, cuts, smallest, high):
    def one(axis_at, blocks):
        heights = jax.random.uniform(jax.random.fold_in(jax.random.fold_in(key, 6), axis_at), (blocks,), jnp.float32, smallest / len(cuts), high / len(cuts))
        return jnp.repeat(jnp.exp(heights), dims[axis_at] // blocks).reshape((-1,) + (1,) * (len(dims) - axis_at - 1))

    loudness = one(*cuts[0])
    for cut in cuts[1:]:
        loudness = loudness * one(*cut)
    return loudness


def noise(rng, dims, scale, bound, pieces=(), held_as=jnp.bfloat16):
    entries = jax.random.normal(rng, dims, jnp.float32) * scale
    if len(pieces) > 0:
        entries = steps_of(rng, dims, pieces, -0.22, 0.18) * entries
    return jnp.clip(entries, min=-bound, max=bound).astype(held_as)


def setup_inputs(seed: int = 0) -> dict:
    keys = jax.random.split(jax.random.key(seed), 6)
    return {
        "left_factor": noise(keys[0], (NAUX, PAIRS), PAIRS ** -0.5, 0.125, ((0, 8), (1, 16)), jnp.float32),
        "right_factor": noise(keys[1], (PAIRS, NAUX), 1.0, 6.0, ((0, 8), (1, 16)), jnp.float32),
        "pair_gap": jnp.clip(jnp.exp(math.log(2.0) - 3.6888794 * jax.random.uniform(keys[2], (PAIRS,), jnp.float32) ** steps_of(keys[2], (PAIRS,), ((0, 16),), -0.2, 0.2)), 0.05, 2.0),
        "mask_left": with_ends((jax.random.randint(keys[3], (NAUX // BLK, PAIRS // BLK), 0, 4) < 1).astype(jnp.int32), jax.random.fold_in(keys[3], 1), 0, 1),
        "mask_right": with_ends((jax.random.randint(keys[4], (PAIRS // BLK, NAUX // BLK), 0, 4) < 1).astype(jnp.int32), jax.random.fold_in(keys[4], 1), 0, 1),
    }


def expand(factor, mask):
    rows, cols = factor.shape
    shaped = factor.reshape(rows // BLK, BLK, cols // BLK, BLK)
    shaped = shaped * mask.astype(jnp.float32)[:, None, :, None]
    return shaped.reshape(rows, cols)


def reference(left_factor, right_factor, pair_gap, mask_left, mask_right):
    weights = jnp.exp(-1.5 * pair_gap)
    scaled_left = expand(left_factor, mask_left) * weights[None, :]
    masked_right = expand(right_factor, mask_right)
    return jnp.dot(scaled_left, masked_right, precision=lax.Precision.HIGHEST, preferred_element_type=jnp.float32)
```

```python
import jax
import jax.numpy as jnp
from jax import lax
from jax.experimental import pallas as pl
from jax.experimental.pallas import tpu as pltpu
from jax.sharding import PartitionSpec as P

BLK = 128
C = 10
E = 4
H = 5
S = C + E
M_STEP = 4
PIECES = ((0, 3), (3, 3), (6, 2), (8, 2))
UP = (0, 3)
AHEAD = 1
COUNT = 127
MESH = pl.DeviceIdType.MESH


def expand(factor, mask):
    rows, cols = factor.shape
    shaped = factor.reshape(rows // BLK, BLK, cols // BLK, BLK)
    shaped = shaped * mask.astype(jnp.float32)[:, None, :, None]
    return shaped.reshape(rows, cols)


def dense_path(left_factor, right_factor, pair_gap, mask_left, mask_right):
    weights = jnp.exp(-1.5 * pair_gap)
    scaled_left = expand(left_factor, mask_left) * weights[None, :]
    masked_right = expand(right_factor, mask_right)

    def place(i, whole):
        part = lax.dynamic_slice(masked_right, (i // 10 * BLK, i % 10 * BLK), (BLK, BLK))
        part = lax.all_gather(part, "row", axis=0, tiled=False)[:, None]
        return lax.dynamic_update_slice(whole, part, (0, i // 10, 0, i % 10 * BLK))

    whole_right = lax.fori_loop(0, 20, place, jnp.zeros((8, 2, BLK, 1280), jnp.float32)).reshape(2048, 1280)

    def rows(i, update):
        part = lax.all_gather(lax.dynamic_slice_in_dim(scaled_left, i * 64, 64, axis=0), "col", axis=1, tiled=True)
        product = jnp.dot(part, whole_right, precision=lax.Precision.HIGHEST, preferred_element_type=jnp.float32)
        return lax.dynamic_update_slice_in_dim(update, product, i * 64, axis=0)

    return lax.fori_loop(0, 40, rows, jnp.zeros((2560, 1280), jnp.float32))


def gather_kernel(
    mask_l, mask_r, gap, left, right,
    split_l, split_r, meta_l, meta_r, flag_out,
    all_l, all_r, far_r, lv, rv, next_l, next_r, out_l, out_r, exc_l, exc_r, got_l, got_r,
    tile, tiles, tile2, tiles2,
    local_sem, send_sem, chunk_l, chunk_r, far_sem, exc_sem, tile_sem, tile2_sem,
):
    r, c = lax.axis_index("row"), lax.axis_index("col")
    z, xl = r // 2, lax.rem(r, 2)
    y, xh, core = c // 4, lax.rem(c // 2, 2), lax.rem(c, 2)

    def col_of(dy, flip_x, flip_core=False):
        return (lax.rem(y + dy, 4) * 2 + (1 - xh if flip_x else xh)) * 2 + (1 - core if flip_core else core)

    def row_of(dz, flip_x):
        return lax.rem(z + dz, 4) * 2 + (1 - xl if flip_x else xl)

    partner = {"row": r, "col": col_of(0, False, True)}
    used = []
    numbers = iter(range(SENDS))

    def send(src, dst, recv_sem, device):
        copy = pltpu.make_async_remote_copy(
            src_ref=src, dst_ref=dst, send_sem=send_sem.at[next(numbers)], recv_sem=recv_sem,
            device_id=device, device_id_type=MESH,
        )
        copy.start()
        used.append(copy)

    def arrived(ref, recv_sem):
        pltpu.make_async_remote_copy(
            src_ref=ref, dst_ref=ref, send_sem=send_sem.at[0], recv_sem=recv_sem,
            device_id=partner, device_id_type=MESH,
        ).wait_recv()

    loads = [pltpu.make_async_copy(left, lv, local_sem.at[0])]
    for j in range(10):
        loads.append(pltpu.make_async_copy(
            right.at[:, pl.ds(j * BLK, BLK)], rv.at[pl.ds(j * 2 * BLK, 2 * BLK), :], local_sem.at[1 + j]))
    for load in loads:
        load.start()

    barrier = pltpu.get_barrier_semaphore()
    for d in range(1, 16):
        pl.semaphore_signal(barrier, inc=1, device_id={"row": r, "col": lax.rem(c + d, 16)}, device_id_type=MESH)
    for d in range(1, 8):
        pl.semaphore_signal(barrier, inc=1, device_id={"row": lax.rem(r + d, 8), "col": c}, device_id_type=MESH)

    def positions(mask_at, nxt):
        nxt[21] = jnp.int32(20)
        nxt[20] = jnp.int32(20)
        following = jnp.int32(20)
        count = jnp.int32(0)
        for b in reversed(range(20)):
            stored = mask_at(b) != 0
            following = jnp.where(stored, jnp.int32(b), following)
            nxt[b] = following
            count = count + jnp.where(stored, 1, 0)
        at = nxt[0]
        found = [at]
        for _ in range(S - 1):
            at = nxt[at + 1]
            found.append(at)
        return found, count

    pos_l, n_l = positions(lambda b: mask_l[b], next_l)
    pos_r, n_r = positions(lambda b: mask_r[b % 2, b // 2], next_r)
    weights = jnp.exp(-1.5 * gap[...])

    def own_l(t):
        return lv[pl.ds(jnp.minimum(pos_l[t], 19) * BLK, BLK), :] * weights

    def own_r(t):
        return rv[pl.ds(jnp.minimum(pos_r[t], 19) * BLK, BLK), :]

    for load in loads:
        load.wait()
    def pack(first, last):
        for t in range(first, last):
            out_l[t] = own_l(t)
            out_r[t] = own_r(t)

    NP = len(PIECES)
    ready = sum(1 for at, size in PIECES if at + size <= C - E)
    pieces = [pl.ds(at, size) for at, size in PIECES]
    ends = [at + size for at, size in PIECES]
    pack(0, ends[0])
    pl.semaphore_wait(barrier, 22)

    up_l, down_l, over_l = ({"row": r, "col": col_of(d, f)} for d, f in ((1, False), (3, False), (0, True)))
    up_r, down_r, over_r = ({"row": row_of(d, f), "col": c} for d, f in ((1, False), (3, False), (0, True)))

    def pass_l(chip_col, h, to, src=None):
        part = all_l.at[chip_col, pieces[h]]
        for device in to:
            send(part if src is None else src, part, chunk_l.at[chip_col, h], device)

    def pass_r(at_row, h, to, src=None):
        part = all_r.at[at_row, pieces[h]]
        for device in to:
            send(part if src is None else src, part, chunk_r.at[at_row, h], device)

    def pass_far(at_row, src=None):
        send(all_r.at[at_row, pl.ds(C - E, E)] if src is None else src, far_r.at[at_row], far_sem.at[at_row], partner)

    def split(block, at, slot):
        high = block.astype(jnp.bfloat16)
        at[slot, :, 0:BLK] = high
        at[slot, :, BLK:] = (block - high.astype(jnp.float32)).astype(jnp.bfloat16)

    def split_piece_l(chip_col, h, src):
        mate = chip_col + 1 - 2 * lax.rem(chip_col, 2)
        first, size = PIECES[h]

        def one(t, _):
            split(src[t], split_l, chip_col * S + t)
            return 0

        lax.fori_loop(first, first + size, one, 0)
        if first >= C - E:
            def other(t, _):
                split(src[t], split_l, mate * S + 2 * C - 1 - t)
                return 0

            lax.fori_loop(first, first + size, other, 0)

    def split_piece_r(at_row, h, src):
        first, size = PIECES[h]

        def one(t, _):
            split(src[t], split_r, at_row * S + t)
            return 0

        lax.fori_loop(first, first + size, one, 0)

    def keep_l(chip_col, h):
        split_piece_l(chip_col, h, all_l.at[chip_col])

    def keep_r(at_row, h):
        split_piece_r(at_row, h, all_r.at[at_row])

    def await_l(chip_col, h):
        arrived(all_l.at[chip_col, pieces[h]], chunk_l.at[chip_col, h])

    def await_r(at_row, h):
        arrived(all_r.at[at_row, pieces[h]], chunk_r.at[at_row, h])

    def from_partner(d, flip, h):
        chip_col = col_of(d, flip, True)
        await_l(chip_col, h)
        keep_l(chip_col, h)

    def far_blocks(d, flip):
        at_row = row_of(d, flip)
        arrived(far_r.at[at_row], far_sem.at[at_row])

        def one(q, _):
            split(far_r[at_row, q], split_r, at_row * S + S - 1 - q)
            return 0

        lax.fori_loop(0, E, one, 0)

    crossing = {}

    def own_piece(h):
        if h < AHEAD:
            cross(h)
        pass_l(c, h, (up_l, down_l), out_l.at[pieces[h]])
        pass_r(r, h, (up_r, down_r), out_r.at[pieces[h]])
        pass_l(c, h, (partner,), out_l.at[pieces[h]])

    def cross(h):
        pass_l(c, h, (over_l,), out_l.at[pieces[h]])
        pass_r(r, h, (over_r,), out_r.at[pieces[h]])
        crossing[h] = used[-2:]

    def cross_after(h):
        for copy in crossing[h - AHEAD]:
            copy.wait_send()
        used[:] = [copy for copy in used if all(copy is not done for done in crossing[h - AHEAD])]
        cross(h)

    own_piece(0)
    for q in range(E):
        exc_l[q] = own_l(C + q)
        exc_r[q] = own_r(C + q)
    send(exc_l, got_l, exc_sem.at[0], partner)
    send(exc_r, got_r, exc_sem.at[1], partner)
    for h in range(1, ready):
        pack(ends[h - 1], ends[h])
        own_piece(h)

    row_at = lax.broadcasted_iota(jnp.int32, (8, BLK), 0)
    lane_at = lax.broadcasted_iota(jnp.int32, (8, BLK), 1)
    note = jnp.where(lane_at == COUNT, jnp.where(row_at == 0, n_l, n_r), 20)
    for t in range(S):
        note = jnp.where(lane_at == t, jnp.where(row_at == 0, pos_l[t], pos_r[t]), note)
    tile[...] = note
    tiles[c] = note
    for d in range(1, 16):
        send(tile, tiles.at[c], tile_sem.at[c], {"row": r, "col": lax.rem(c + d, 16)})

    arrived(got_l, exc_sem.at[0])
    arrived(got_r, exc_sem.at[1])
    pack(ends[ready - 1], C - E)
    for t in range(C - E, C):
        out_l[t] = jnp.where(t < n_l, own_l(t), got_l[C - 1 - t])
        out_r[t] = jnp.where(t < n_r, own_r(t), got_r[C - 1 - t])
    for h in range(ready, NP):
        own_piece(h)
    pass_far(r, out_r.at[pl.ds(C - E, E)])
    def keep_own():
        for h in range(NP):
            split_piece_l(c, h, out_l)
            split_piece_r(r, h, out_r)

    def lists_l():
        for d in range(1, 16):
            other = lax.rem(c + d, 16)
            arrived(tiles.at[other], tile_sem.at[other])
        over = jnp.zeros((8, BLK), jnp.int32)
        for pair in range(8):
            one, two = tiles[2 * pair], tiles[2 * pair + 1]
            meta_l[pl.ds(2 * pair, 1), :] = one[0:1]
            meta_l[pl.ds(2 * pair + 1, 1), :] = two[0:1]
            full = jnp.where((one > C + E) | (two > C + E) | (one + two > 2 * C), 1, 0)
            over = jnp.maximum(over, full)
        over = jnp.where(lane_at == COUNT, over, 0)
        over = jnp.maximum(over[0:1], over[1:2])
        note2 = jnp.where(row_at == 0, note[1:2], over)
        tile2[...] = note2
        tiles2[r] = note2
        for d in range(1, 8):
            send(tile2, tiles2.at[r], tile2_sem.at[r], {"row": lax.rem(r + d, 8), "col": c})

    def lists_r():
        for d in range(1, 8):
            other = lax.rem(r + d, 8)
            arrived(tiles2.at[other], tile2_sem.at[other])
        flag = jnp.zeros((1, BLK), jnp.int32)
        for k in range(8):
            got = tiles2[k]
            meta_r[pl.ds(k, 1), :] = got[0:1]
            flag = jnp.maximum(flag, got[1:2])
        flag_out[...] = jnp.broadcast_to(flag, (8, BLK))

    def from_x(h):
        mine_l, mine_r = col_of(0, True), row_of(0, True)
        await_r(mine_r, h)
        pass_r(mine_r, h, (up_r, down_r))
        await_l(mine_l, h)
        pass_l(mine_l, h, (up_l, down_l, partner))
        if h == NP - 1:
            pass_far(mine_r)
        keep_r(mine_r, h)
        keep_l(mine_l, h)

    def from_ring(flip, h):
        for d in (3, 1):
            onward = (h in UP) == (d == 3)
            await_l(col_of(d, flip), h)
            pass_l(col_of(d, flip), h, (((up_l if d == 3 else down_l),) if onward else ()) + (partner,))
            await_r(row_of(d, flip), h)
            pass_r(row_of(d, flip), h, ((up_r if d == 3 else down_r),) if onward else ())
            if h == NP - 1:
                pass_far(row_of(d, flip))
        for d in (3, 1):
            keep_l(col_of(d, flip), h)
            keep_r(row_of(d, flip), h)

    def from_far(flip, h):
        await_l(col_of(2, flip), h)
        pass_l(col_of(2, flip), h, (partner,))
        await_r(row_of(2, flip), h)
        if h == NP - 1:
            pass_far(row_of(2, flip))
        keep_l(col_of(2, flip), h)
        keep_r(row_of(2, flip), h)

    events = [(0.12, keep_own, ()), (0.3, lists_l, ()), (1.1, lists_r, ())]
    for h in range(NP):
        share = ends[h] / C
        if h >= AHEAD:
            events.append((2 * ends[h - AHEAD] / C - 0.02, cross_after, (h,)))
        ring, x, far = share, 2 * share, 1 + share
        ring2, far2 = max(1.5, 2 * share) + share / 2 + 0.2, 3 + share
        events.append((ring, from_ring, (False, h)))
        events.append((x, from_x, (h,)))
        events.append((far, from_far, (False, h)))
        events.append((ring2, from_ring, (True, h)))
        events.append((far2, from_far, (True, h)))
        events.append((0.26 + share / 2, from_partner, (0, False, h)))
        for d in (1, 3):
            events.append((ring + 0.3, from_partner, (d, False, h)))
            events.append((ring2 + 0.3, from_partner, (d, True, h)))
        events.append((x + 0.3, from_partner, (0, True, h)))
        events.append((far + 0.3, from_partner, (2, False, h)))
        events.append((far2 + 0.3, from_partner, (2, True, h)))
    for d in range(4):
        for flip in (False, True):
            events.append(((1 if d == 0 else 2) + 1.1 + flip * 0.9 + 0.3 * d, far_blocks, (d, flip)))
    for _, what, how in sorted(events, key=lambda event: event[0]):
        what(*how)
    for copy in used:
        copy.wait_send()


SENDS = 136


def gather(left_factor, right_factor, pair_gap, mask_left, mask_right):
    smem = pl.BlockSpec(memory_space=pltpu.SMEM)
    vmem = pl.BlockSpec(memory_space=pltpu.VMEM)
    hbm = pl.BlockSpec(memory_space=pl.ANY)
    f32, i32 = jnp.float32, jnp.int32
    dma = pltpu.SemaphoreType.DMA
    return pl.pallas_call(
        gather_kernel,
        out_shape=(
            jax.ShapeDtypeStruct((16 * S + M_STEP, BLK, 2 * BLK), jnp.bfloat16),
            jax.ShapeDtypeStruct((8 * S, BLK, 2 * BLK), jnp.bfloat16),
            jax.ShapeDtypeStruct((16, BLK), i32),
            jax.ShapeDtypeStruct((8, BLK), i32),
            jax.ShapeDtypeStruct((8, BLK), i32),
        ),
        in_specs=[smem, smem, vmem, hbm, hbm],
        out_specs=(vmem,) * 5,
        scratch_shapes=[
            pltpu.VMEM((16, C, BLK, BLK), f32), pltpu.VMEM((8, C, BLK, BLK), f32), pltpu.VMEM((8, E, BLK, BLK), f32),
            pltpu.VMEM((20 * BLK, BLK), f32), pltpu.VMEM((20 * BLK, BLK), f32),
            pltpu.SMEM((22,), i32), pltpu.SMEM((22,), i32),
            pltpu.VMEM((C, BLK, BLK), f32), pltpu.VMEM((C, BLK, BLK), f32),
            pltpu.VMEM((E, BLK, BLK), f32), pltpu.VMEM((E, BLK, BLK), f32),
            pltpu.VMEM((E, BLK, BLK), f32), pltpu.VMEM((E, BLK, BLK), f32),
            pltpu.VMEM((8, BLK), i32), pltpu.VMEM((16, 8, BLK), i32),
            pltpu.VMEM((8, BLK), i32), pltpu.VMEM((8, 8, BLK), i32),
            dma((13,)), dma((SENDS,)), dma((16, len(PIECES))), dma((8, len(PIECES))), dma((8,)), dma((2,)), dma((16,)), dma((8,)),
        ],
        compiler_params=pltpu.CompilerParams(
            collective_id=0, has_side_effects=True, vmem_limit_bytes=30 << 20),
    )(mask_left.reshape(20), mask_right, pair_gap.reshape(1, BLK), left_factor, right_factor)


W = 12
ENTRIES = 16 * 5 * 5 + 2


def product_kernel(meta_l, meta_r, split_l, split_r, update, acc, slot_of, strip_of, left_of, right_of, sem_o):
    def count(meta, at):
        return jnp.minimum(meta[at, COUNT], S)

    def zero(i, _):
        rows = pl.ds(pl.multiple_of(lax.rem(i, 10) * 256, 256), 256)
        acc[i // 10, rows, :] = jnp.zeros((256, BLK), jnp.float32)
        return 0

    lax.fori_loop(0, 100, zero, 0)

    def clear(i, _):
        slot_of[i] = jnp.int32(0)
        strip_of[i] = jnp.int32(10)
        return 0

    lax.fori_loop(0, 17 * W, clear, 0, unroll=6)

    def sort_r(k, total):
        def one(t, ends):
            b = meta_r[k, t]
            odd = lax.rem(b, 2)
            place = (2 * k + odd) * W + jnp.where(odd == 1, ends[1], ends[0])
            slot_of[place] = k * S + t
            strip_of[place] = b // 2
            return ends[0] + 1 - odd, ends[1] + odd

        ends = lax.fori_loop(0, count(meta_r, k), one, (jnp.int32(0), jnp.int32(0)))
        for odd in range(2):
            pair = 2 * k + odd
            steps = (count(meta_l, pair) + M_STEP - 1) // M_STEP

            def across(q, total):
                def down(u, total):
                    left_of[total] = pair * 4 + u
                    right_of[total] = pair * W + 2 * q
                    return total + 1

                return lax.fori_loop(0, steps, down, total)

            total = lax.fori_loop(0, (ends[odd] + 1) // 2, across, total)
        return total

    total = lax.fori_loop(0, 8, sort_r, jnp.int32(0))
    left_of[total] = jnp.int32(0)
    right_of[total] = jnp.int32(16 * W)

    def step(n):
        at_l, at_r = left_of[n], right_of[n]
        k, u = at_l // 4, lax.rem(at_l, 4)
        one, two = split_r[slot_of[at_r]], split_r[slot_of[at_r + 1]]
        highs = jnp.concatenate([one[:, :BLK], two[:, :BLK]], axis=1)
        lows = jnp.concatenate([one[:, BLK:], two[:, BLK:]], axis=1)
        weights = jnp.concatenate([highs, highs, lows], axis=0)
        lhs = split_l[pl.ds(k * S + u * M_STEP, M_STEP)].reshape(M_STEP * BLK, 2 * BLK)
        lhs = jnp.concatenate([lhs, lhs[:, :BLK]], axis=1)
        return k, u, at_r, jnp.dot(lhs, weights, preferred_element_type=jnp.float32)

    def store(k, u, at_r, full):
        for v in range(M_STEP):
            rows = pl.ds(pl.multiple_of(meta_l[k, u * M_STEP + v] * BLK, BLK), BLK)
            for w in range(2):
                acc[strip_of[at_r + w], rows, :] += full[v * BLK:(v + 1) * BLK, w * BLK:(w + 1) * BLK]

    def two_steps(n, _):
        first = step(2 * n)
        second = step(2 * n + 1)
        store(*first)
        store(*second)
        return 0

    lax.fori_loop(0, (total + 1) // 2, two_steps, 0)

    outs = [
        pltpu.make_async_copy(acc.at[j, pl.ds(0, 20 * BLK)], update.at[:, pl.ds(j * BLK, BLK)], sem_o.at[j])
        for j in range(10)
    ]
    for copy in outs:
        copy.start()
    for copy in outs:
        copy.wait()


def product(meta_l, meta_r, split_l, split_r):
    smem = pl.BlockSpec(memory_space=pltpu.SMEM)
    vmem = pl.BlockSpec(memory_space=pltpu.VMEM)
    f32, i32 = jnp.float32, jnp.int32
    return pl.pallas_call(
        product_kernel,
        out_shape=jax.ShapeDtypeStruct((20 * BLK, 10 * BLK), f32),
        in_specs=[smem, smem, vmem, vmem],
        out_specs=pl.BlockSpec(memory_space=pl.ANY),
        scratch_shapes=[
            pltpu.VMEM((11, 21 * BLK, BLK), f32),
            pltpu.SMEM((17 * W,), i32), pltpu.SMEM((17 * W,), i32),
            pltpu.SMEM((ENTRIES,), i32), pltpu.SMEM((ENTRIES,), i32),
            pltpu.SemaphoreType.DMA((10,)),
        ],
        compiler_params=pltpu.CompilerParams(vmem_limit_bytes=24 << 20),
    )(meta_l, meta_r, split_l, split_r)


def per_device(left_factor, right_factor, pair_gap, mask_left, mask_right):
    split_l, split_r, meta_l, meta_r, flag = gather(left_factor, right_factor, pair_gap, mask_left, mask_right)
    return lax.cond(
        flag[0, COUNT] > 0,
        lambda: dense_path(left_factor, right_factor, pair_gap, mask_left, mask_right),
        lambda: product(meta_l, meta_r, split_l, split_r),
    )


def solution(mesh):
    return jax.shard_map(
        per_device,
        mesh=mesh,
        in_specs=(P("row", "col"), P("row", "col"), P("col"), P("row", "col"), P("row", "col")),
        out_specs=P("row", "col"),
        check_vma=False,
    )
```

```python
import jax
import jax.numpy as jnp
from jax import lax
from jax.experimental import pallas as pl
from jax.experimental.pallas import tpu as pltpu
from jax.sharding import PartitionSpec as P

BLK = 128
C = 10
E = 4
H = 5
S = C + E
M_STEP = 7
PIECES = ((0, 3), (3, 3), (6, 2), (8, 2))
UP = (0, 3)
AHEAD = 1
COUNT = 127
MESH = pl.DeviceIdType.MESH


def expand(factor, mask):
    rows, cols = factor.shape
    shaped = factor.reshape(rows // BLK, BLK, cols // BLK, BLK)
    shaped = shaped * mask.astype(jnp.float32)[:, None, :, None]
    return shaped.reshape(rows, cols)


def dense_path(left_factor, right_factor, pair_gap, mask_left, mask_right):
    weights = jnp.exp(-1.5 * pair_gap)
    scaled_left = expand(left_factor, mask_left) * weights[None, :]
    masked_right = expand(right_factor, mask_right)

    def place(i, whole):
        part = lax.dynamic_slice(masked_right, (i // 10 * BLK, i % 10 * BLK), (BLK, BLK))
        part = lax.all_gather(part, "row", axis=0, tiled=False)[:, None]
        return lax.dynamic_update_slice(whole, part, (0, i // 10, 0, i % 10 * BLK))

    whole_right = lax.fori_loop(0, 20, place, jnp.zeros((8, 2, BLK, 1280), jnp.float32)).reshape(2048, 1280)

    def rows(i, update):
        part = lax.all_gather(lax.dynamic_slice_in_dim(scaled_left, i * 64, 64, axis=0), "col", axis=1, tiled=True)
        product = jnp.dot(part, whole_right, precision=lax.Precision.HIGHEST, preferred_element_type=jnp.float32)
        return lax.dynamic_update_slice_in_dim(update, product, i * 64, axis=0)

    return lax.fori_loop(0, 40, rows, jnp.zeros((2560, 1280), jnp.float32))


def gather_kernel(
    mask_l, mask_r, gap, left, right,
    split_l, split_r, meta_l, meta_r, flag_out,
    all_l, all_r, far_r, lv, rv, next_l, next_r, out_l, out_r, exc_l, exc_r, got_l, got_r,
    tile, tiles, tile2, tiles2,
    local_sem, send_sem, chunk_l, chunk_r, far_sem, exc_sem, tile_sem, tile2_sem,
):
    r, c = lax.axis_index("row"), lax.axis_index("col")
    z, xl = r // 2, lax.rem(r, 2)
    y, xh, core = c // 4, lax.rem(c // 2, 2), lax.rem(c, 2)

    def col_of(dy, flip_x, flip_core=False):
        return (lax.rem(y + dy, 4) * 2 + (1 - xh if flip_x else xh)) * 2 + (1 - core if flip_core else core)

    def row_of(dz, flip_x):
        return lax.rem(z + dz, 4) * 2 + (1 - xl if flip_x else xl)

    partner = {"row": r, "col": col_of(0, False, True)}
    used = []
    numbers = iter(range(SENDS))

    def send(src, dst, recv_sem, device):
        copy = pltpu.make_async_remote_copy(
            src_ref=src, dst_ref=dst, send_sem=send_sem.at[next(numbers)], recv_sem=recv_sem,
            device_id=device, device_id_type=MESH,
        )
        copy.start()
        used.append(copy)

    def arrived(ref, recv_sem):
        pltpu.make_async_remote_copy(
            src_ref=ref, dst_ref=ref, send_sem=send_sem.at[0], recv_sem=recv_sem,
            device_id=partner, device_id_type=MESH,
        ).wait_recv()

    loads = [pltpu.make_async_copy(left, lv, local_sem.at[0])]
    for j in range(10):
        loads.append(pltpu.make_async_copy(
            right.at[:, pl.ds(j * BLK, BLK)], rv.at[pl.ds(j * 2 * BLK, 2 * BLK), :], local_sem.at[1 + j]))
    for load in loads:
        load.start()

    barrier = pltpu.get_barrier_semaphore()
    for d in range(1, 16):
        pl.semaphore_signal(barrier, inc=1, device_id={"row": r, "col": lax.rem(c + d, 16)}, device_id_type=MESH)
    for d in range(1, 8):
        pl.semaphore_signal(barrier, inc=1, device_id={"row": lax.rem(r + d, 8), "col": c}, device_id_type=MESH)

    def positions(mask_at, nxt):
        nxt[21] = jnp.int32(20)
        nxt[20] = jnp.int32(20)
        following = jnp.int32(20)
        count = jnp.int32(0)
        for b in reversed(range(20)):
            stored = mask_at(b) != 0
            following = jnp.where(stored, jnp.int32(b), following)
            nxt[b] = following
            count = count + jnp.where(stored, 1, 0)
        at = nxt[0]
        found = [at]
        for _ in range(S - 1):
            at = nxt[at + 1]
            found.append(at)
        return found, count

    pos_l, n_l = positions(lambda b: mask_l[b], next_l)
    pos_r, n_r = positions(lambda b: mask_r[b % 2, b // 2], next_r)
    weights = jnp.exp(-1.5 * gap[...])

    def own_l(t):
        return lv[pl.ds(jnp.minimum(pos_l[t], 19) * BLK, BLK), :] * weights

    def own_r(t):
        return rv[pl.ds(jnp.minimum(pos_r[t], 19) * BLK, BLK), :]

    for load in loads:
        load.wait()
    def pack(first, last):
        for t in range(first, last):
            out_l[t] = own_l(t)
            out_r[t] = own_r(t)

    NP = len(PIECES)
    ready = sum(1 for at, size in PIECES if at + size <= C - E)
    pieces = [pl.ds(at, size) for at, size in PIECES]
    ends = [at + size for at, size in PIECES]
    pack(0, ends[0])
    pl.semaphore_wait(barrier, 22)

    up_l, down_l, over_l = ({"row": r, "col": col_of(d, f)} for d, f in ((1, False), (3, False), (0, True)))
    up_r, down_r, over_r = ({"row": row_of(d, f), "col": c} for d, f in ((1, False), (3, False), (0, True)))

    def pass_l(chip_col, h, to, src=None):
        part = all_l.at[chip_col, pieces[h]]
        for device in to:
            send(part if src is None else src, part, chunk_l.at[chip_col, h], device)

    def pass_r(at_row, h, to, src=None):
        part = all_r.at[at_row, pieces[h]]
        for device in to:
            send(part if src is None else src, part, chunk_r.at[at_row, h], device)

    def pass_far(at_row, src=None):
        send(all_r.at[at_row, pl.ds(C - E, E)] if src is None else src, far_r.at[at_row], far_sem.at[at_row], partner)

    def split(block, at, slot):
        high = block.astype(jnp.bfloat16)
        at[slot, :, 0:BLK] = high
        at[slot, :, BLK:] = (block - high.astype(jnp.float32)).astype(jnp.bfloat16)

    def split_piece_l(chip_col, h, src):
        mate = chip_col + 1 - 2 * lax.rem(chip_col, 2)
        first, size = PIECES[h]

        def one(t, _):
            split(src[t], split_l, chip_col * S + t)
            return 0

        lax.fori_loop(first, first + size, one, 0)
        if first >= C - E:
            def other(t, _):
                split(src[t], split_l, mate * S + 2 * C - 1 - t)
                return 0

            lax.fori_loop(first, first + size, other, 0)

    def split_piece_r(at_row, h, src):
        first, size = PIECES[h]

        def one(t, _):
            split(src[t], split_r, at_row * S + t)
            return 0

        lax.fori_loop(first, first + size, one, 0)

    def keep_l(chip_col, h):
        split_piece_l(chip_col, h, all_l.at[chip_col])

    def keep_r(at_row, h):
        split_piece_r(at_row, h, all_r.at[at_row])

    def await_l(chip_col, h):
        arrived(all_l.at[chip_col, pieces[h]], chunk_l.at[chip_col, h])

    def await_r(at_row, h):
        arrived(all_r.at[at_row, pieces[h]], chunk_r.at[at_row, h])

    def from_partner(d, flip, h):
        chip_col = col_of(d, flip, True)
        await_l(chip_col, h)
        keep_l(chip_col, h)

    def far_blocks(d, flip):
        at_row = row_of(d, flip)
        arrived(far_r.at[at_row], far_sem.at[at_row])

        def one(q, _):
            split(far_r[at_row, q], split_r, at_row * S + S - 1 - q)
            return 0

        lax.fori_loop(0, E, one, 0)

    crossing = {}

    def own_piece(h):
        if h < AHEAD:
            cross(h)
        pass_l(c, h, (up_l, down_l), out_l.at[pieces[h]])
        pass_r(r, h, (up_r, down_r), out_r.at[pieces[h]])
        pass_l(c, h, (partner,), out_l.at[pieces[h]])

    def cross(h):
        pass_l(c, h, (over_l,), out_l.at[pieces[h]])
        pass_r(r, h, (over_r,), out_r.at[pieces[h]])
        crossing[h] = used[-2:]

    def cross_after(h):
        for copy in crossing[h - AHEAD]:
            copy.wait_send()
        used[:] = [copy for copy in used if all(copy is not done for done in crossing[h - AHEAD])]
        cross(h)

    own_piece(0)
    for q in range(E):
        exc_l[q] = own_l(C + q)
        exc_r[q] = own_r(C + q)
    send(exc_l, got_l, exc_sem.at[0], partner)
    send(exc_r, got_r, exc_sem.at[1], partner)
    for h in range(1, ready):
        pack(ends[h - 1], ends[h])
        own_piece(h)

    row_at = lax.broadcasted_iota(jnp.int32, (8, BLK), 0)
    lane_at = lax.broadcasted_iota(jnp.int32, (8, BLK), 1)
    note = jnp.where(lane_at == COUNT, jnp.where(row_at == 0, n_l, n_r), 20)
    for t in range(S):
        note = jnp.where(lane_at == t, jnp.where(row_at == 0, pos_l[t], pos_r[t]), note)
    tile[...] = note
    tiles[c] = note
    for d in range(1, 16):
        send(tile, tiles.at[c], tile_sem.at[c], {"row": r, "col": lax.rem(c + d, 16)})

    arrived(got_l, exc_sem.at[0])
    arrived(got_r, exc_sem.at[1])
    pack(ends[ready - 1], C - E)
    for t in range(C - E, C):
        out_l[t] = jnp.where(t < n_l, own_l(t), got_l[C - 1 - t])
        out_r[t] = jnp.where(t < n_r, own_r(t), got_r[C - 1 - t])
    for h in range(ready, NP):
        own_piece(h)
    pass_far(r, out_r.at[pl.ds(C - E, E)])
    def keep_own():
        for h in range(NP):
            split_piece_l(c, h, out_l)
            split_piece_r(r, h, out_r)

    def lists_l():
        for d in range(1, 16):
            other = lax.rem(c + d, 16)
            arrived(tiles.at[other], tile_sem.at[other])
        over = jnp.zeros((8, BLK), jnp.int32)
        for pair in range(8):
            one, two = tiles[2 * pair], tiles[2 * pair + 1]
            meta_l[pl.ds(2 * pair, 1), :] = one[0:1]
            meta_l[pl.ds(2 * pair + 1, 1), :] = two[0:1]
            full = jnp.where((one > C + E) | (two > C + E) | (one + two > 2 * C), 1, 0)
            over = jnp.maximum(over, full)
        over = jnp.where(lane_at == COUNT, over, 0)
        over = jnp.maximum(over[0:1], over[1:2])
        note2 = jnp.where(row_at == 0, note[1:2], over)
        tile2[...] = note2
        tiles2[r] = note2
        for d in range(1, 8):
            send(tile2, tiles2.at[r], tile2_sem.at[r], {"row": lax.rem(r + d, 8), "col": c})

    def lists_r():
        for d in range(1, 8):
            other = lax.rem(r + d, 8)
            arrived(tiles2.at[other], tile2_sem.at[other])
        flag = jnp.zeros((1, BLK), jnp.int32)
        for k in range(8):
            got = tiles2[k]
            meta_r[pl.ds(k, 1), :] = got[0:1]
            flag = jnp.maximum(flag, got[1:2])
        flag_out[...] = jnp.broadcast_to(flag, (8, BLK))

    def from_x(h):
        mine_l, mine_r = col_of(0, True), row_of(0, True)
        await_r(mine_r, h)
        pass_r(mine_r, h, (up_r, down_r))
        await_l(mine_l, h)
        pass_l(mine_l, h, (up_l, down_l, partner))
        if h == NP - 1:
            pass_far(mine_r)
        keep_r(mine_r, h)
        keep_l(mine_l, h)

    def from_ring(flip, h):
        for d in (3, 1):
            onward = (h in UP) == (d == 3)
            await_l(col_of(d, flip), h)
            pass_l(col_of(d, flip), h, (((up_l if d == 3 else down_l),) if onward else ()) + (partner,))
            await_r(row_of(d, flip), h)
            pass_r(row_of(d, flip), h, ((up_r if d == 3 else down_r),) if onward else ())
            if h == NP - 1:
                pass_far(row_of(d, flip))
        for d in (3, 1):
            keep_l(col_of(d, flip), h)
            keep_r(row_of(d, flip), h)

    def from_far(flip, h):
        await_l(col_of(2, flip), h)
        pass_l(col_of(2, flip), h, (partner,))
        await_r(row_of(2, flip), h)
        if h == NP - 1:
            pass_far(row_of(2, flip))
        keep_l(col_of(2, flip), h)
        keep_r(row_of(2, flip), h)

    events = [(0.12, keep_own, ()), (0.3, lists_l, ()), (1.1, lists_r, ())]
    for h in range(NP):
        share = ends[h] / C
        if h >= AHEAD:
            events.append((2 * ends[h - AHEAD] / C - 0.02, cross_after, (h,)))
        ring, x, far = share, 2 * share, 1 + share
        ring2, far2 = max(1.5, 2 * share) + share / 2 + 0.2, 3 + share
        events.append((ring, from_ring, (False, h)))
        events.append((x, from_x, (h,)))
        events.append((far, from_far, (False, h)))
        events.append((ring2, from_ring, (True, h)))
        events.append((far2, from_far, (True, h)))
        events.append((0.26 + share / 2, from_partner, (0, False, h)))
        for d in (1, 3):
            events.append((ring + 0.3, from_partner, (d, False, h)))
            events.append((ring2 + 0.3, from_partner, (d, True, h)))
        events.append((x + 0.3, from_partner, (0, True, h)))
        events.append((far + 0.3, from_partner, (2, False, h)))
        events.append((far2 + 0.3, from_partner, (2, True, h)))
    for d in range(4):
        for flip in (False, True):
            events.append(((1 if d == 0 else 2) + 1.1 + flip * 0.9 + 0.3 * d, far_blocks, (d, flip)))
    for _, what, how in sorted(events, key=lambda event: event[0]):
        what(*how)
    for copy in used:
        copy.wait_send()


SENDS = 136


def gather(left_factor, right_factor, pair_gap, mask_left, mask_right):
    smem = pl.BlockSpec(memory_space=pltpu.SMEM)
    vmem = pl.BlockSpec(memory_space=pltpu.VMEM)
    hbm = pl.BlockSpec(memory_space=pl.ANY)
    f32, i32 = jnp.float32, jnp.int32
    dma = pltpu.SemaphoreType.DMA
    return pl.pallas_call(
        gather_kernel,
        out_shape=(
            jax.ShapeDtypeStruct((16 * S + M_STEP, BLK, 2 * BLK), jnp.bfloat16),
            jax.ShapeDtypeStruct((8 * S, BLK, 2 * BLK), jnp.bfloat16),
            jax.ShapeDtypeStruct((16, BLK), i32),
            jax.ShapeDtypeStruct((8, BLK), i32),
            jax.ShapeDtypeStruct((8, BLK), i32),
        ),
        in_specs=[smem, smem, vmem, hbm, hbm],
        out_specs=(vmem,) * 5,
        scratch_shapes=[
            pltpu.VMEM((16, C, BLK, BLK), f32), pltpu.VMEM((8, C, BLK, BLK), f32), pltpu.VMEM((8, E, BLK, BLK), f32),
            pltpu.VMEM((20 * BLK, BLK), f32), pltpu.VMEM((20 * BLK, BLK), f32),
            pltpu.SMEM((22,), i32), pltpu.SMEM((22,), i32),
            pltpu.VMEM((C, BLK, BLK), f32), pltpu.VMEM((C, BLK, BLK), f32),
            pltpu.VMEM((E, BLK, BLK), f32), pltpu.VMEM((E, BLK, BLK), f32),
            pltpu.VMEM((E, BLK, BLK), f32), pltpu.VMEM((E, BLK, BLK), f32),
            pltpu.VMEM((8, BLK), i32), pltpu.VMEM((16, 8, BLK), i32),
            pltpu.VMEM((8, BLK), i32), pltpu.VMEM((8, 8, BLK), i32),
            dma((13,)), dma((SENDS,)), dma((16, len(PIECES))), dma((8, len(PIECES))), dma((8,)), dma((2,)), dma((16,)), dma((8,)),
        ],
        compiler_params=pltpu.CompilerParams(
            collective_id=0, has_side_effects=True, vmem_limit_bytes=30 << 20),
    )(mask_left.reshape(20), mask_right, pair_gap.reshape(1, BLK), left_factor, right_factor)


CUTS = (8, 12, 14, 15, 16)
W = 12
ENTRIES = 16 * 5 * 5 + 2


def product_kernel(meta_l, meta_r, split_l, split_r, update, acc, slot_of, strip_of, left_of, right_of, steps_of, last_of, sem_o):
    def count(meta, at):
        return jnp.minimum(meta[at, COUNT], S)

    def zero(i, _):
        rows = pl.ds(pl.multiple_of(lax.rem(i, 10) * 256, 256), 256)
        acc[i // 10, rows, :] = jnp.zeros((256, BLK), jnp.float32)
        for n in (2 * i, 2 * i + 1):
            slot_of[n] = jnp.int32(0)
            strip_of[n] = jnp.int32(10)
        return 0

    lax.fori_loop(0, 17 * W // 2, zero, 0)
    for j in range(10):
        last_of[j] = jnp.int32(-1)

    def sort_r(k, total):
        def one(t, ends):
            b = meta_r[k, t]
            odd = lax.rem(b, 2)
            place = (2 * k + odd) * W + jnp.where(odd == 1, ends[1], ends[0])
            slot_of[place] = k * S + t
            strip_of[place] = b // 2
            last_of[b // 2] = 2 * k + odd
            return ends[0] + 1 - odd, ends[1] + odd

        ends = lax.fori_loop(0, count(meta_r, k), one, (jnp.int32(0), jnp.int32(0)))
        for odd in range(2):
            pair = 2 * k + odd
            steps = (count(meta_l, pair) + M_STEP - 1) // M_STEP

            def across(q, total):
                def down(u, total):
                    left_of[total] = pair * 4 + u
                    right_of[total] = pair * W + 2 * q
                    return total + 1

                return lax.fori_loop(0, steps, down, total)

            total = lax.fori_loop(0, (ends[odd] + 1) // 2, across, total)
            steps_of[pair] = total
        return total

    total = lax.fori_loop(0, 8, sort_r, jnp.int32(0))
    left_of[total] = jnp.int32(0)
    right_of[total] = jnp.int32(16 * W)

    def step(n):
        at_l, at_r = left_of[n], right_of[n]
        k, u = at_l // 4, lax.rem(at_l, 4)
        one, two = split_r[slot_of[at_r]], split_r[slot_of[at_r + 1]]
        highs = jnp.concatenate([one[:, :BLK], two[:, :BLK]], axis=1)
        lows = jnp.concatenate([one[:, BLK:], two[:, BLK:]], axis=1)
        weights = jnp.concatenate([highs, highs, lows], axis=0)
        lhs = split_l[pl.ds(k * S + u * M_STEP, M_STEP)].reshape(M_STEP * BLK, 2 * BLK)
        lhs = jnp.concatenate([lhs, lhs[:, :BLK]], axis=1)
        return k, u, at_r, jnp.dot(lhs, weights, preferred_element_type=jnp.float32)

    def store(k, u, at_r, full):
        for v in range(M_STEP):
            rows = pl.ds(pl.multiple_of(meta_l[k, u * M_STEP + v] * BLK, BLK), BLK)
            for w in range(2):
                acc[strip_of[at_r + w], rows, :] += full[v * BLK:(v + 1) * BLK, w * BLK:(w + 1) * BLK]

    def two_steps(n, _):
        first = step(2 * n)
        second = step(2 * n + 1)
        store(*first)
        store(*second)
        return 0

    outs = [
        pltpu.make_async_copy(acc.at[j, pl.ds(0, 20 * BLK)], update.at[:, pl.ds(j * BLK, BLK)], sem_o.at[j])
        for j in range(10)
    ]
    done, before = jnp.int32(0), -1
    for pairs in CUTS:
        now = (steps_of[pairs - 1] + 1) // 2
        lax.fori_loop(done, now, two_steps, 0)
        for j in range(10):
            last = last_of[j]

            @pl.when((last >= before) & (last < pairs))
            def _():
                outs[j].start()

        done, before = now, pairs
    for copy in outs:
        copy.wait()


def product(meta_l, meta_r, split_l, split_r):
    smem = pl.BlockSpec(memory_space=pltpu.SMEM)
    vmem = pl.BlockSpec(memory_space=pltpu.VMEM)
    f32, i32 = jnp.float32, jnp.int32
    return pl.pallas_call(
        product_kernel,
        out_shape=jax.ShapeDtypeStruct((20 * BLK, 10 * BLK), f32),
        in_specs=[smem, smem, vmem, vmem],
        out_specs=pl.BlockSpec(memory_space=pl.ANY),
        scratch_shapes=[
            pltpu.VMEM((11, 21 * BLK, BLK), f32),
            pltpu.SMEM((17 * W,), i32), pltpu.SMEM((17 * W,), i32),
            pltpu.SMEM((ENTRIES,), i32), pltpu.SMEM((ENTRIES,), i32),
            pltpu.SMEM((16,), i32), pltpu.SMEM((10,), i32),
            pltpu.SemaphoreType.DMA((10,)),
        ],
        compiler_params=pltpu.CompilerParams(vmem_limit_bytes=24 << 20),
    )(meta_l, meta_r, split_l, split_r)


def per_device(left_factor, right_factor, pair_gap, mask_left, mask_right):
    split_l, split_r, meta_l, meta_r, flag = gather(left_factor, right_factor, pair_gap, mask_left, mask_right)
    return lax.cond(
        flag[0, COUNT] > 0,
        lambda: dense_path(left_factor, right_factor, pair_gap, mask_left, mask_right),
        lambda: product(meta_l, meta_r, split_l, split_r),
    )


def solution(mesh):
    return jax.shard_map(
        per_device,
        mesh=mesh,
        in_specs=(P("row", "col"), P("row", "col"), P("col"), P("row", "col"), P("row", "col")),
        out_specs=P("row", "col"),
        check_vma=False,
    )
```

```python
import jax
import jax.numpy as jnp
from jax import lax
from jax.experimental import pallas as pl
from jax.experimental.pallas import tpu as pltpu
from jax.sharding import PartitionSpec as P

BLK = 128
C = 10
E = 4
H = 5
S = C + E
M_STEP = 7
PIECES = ((0, 3), (3, 3), (6, 2), (8, 2))
UP = (0, 3)
AHEAD = 1
COUNT = 127
MESH = pl.DeviceIdType.MESH


def expand(factor, mask):
    rows, cols = factor.shape
    shaped = factor.reshape(rows // BLK, BLK, cols // BLK, BLK)
    shaped = shaped * mask.astype(jnp.float32)[:, None, :, None]
    return shaped.reshape(rows, cols)


def dense_path(left_factor, right_factor, pair_gap, mask_left, mask_right):
    weights = jnp.exp(-1.5 * pair_gap)
    scaled_left = expand(left_factor, mask_left) * weights[None, :]
    masked_right = expand(right_factor, mask_right)

    def place(i, whole):
        part = lax.dynamic_slice(masked_right, (i // 10 * BLK, i % 10 * BLK), (BLK, BLK))
        part = lax.all_gather(part, "row", axis=0, tiled=False)[:, None]
        return lax.dynamic_update_slice(whole, part, (0, i // 10, 0, i % 10 * BLK))

    whole_right = lax.fori_loop(0, 20, place, jnp.zeros((8, 2, BLK, 1280), jnp.float32)).reshape(2048, 1280)

    def rows(i, update):
        part = lax.all_gather(lax.dynamic_slice_in_dim(scaled_left, i * 64, 64, axis=0), "col", axis=1, tiled=True)
        product = jnp.dot(part, whole_right, precision=lax.Precision.HIGHEST, preferred_element_type=jnp.float32)
        return lax.dynamic_update_slice_in_dim(update, product, i * 64, axis=0)

    return lax.fori_loop(0, 40, rows, jnp.zeros((2560, 1280), jnp.float32))


def gather_kernel(
    mask_l, mask_r, gap, left, right,
    split_l, split_r, meta_l, meta_r, flag_out,
    all_l, all_r, far_r, lv, rv, next_l, next_r, out_l, out_r, exc_l, exc_r, got_l, got_r,
    tile, tiles, tile2, tiles2,
    local_sem, send_sem, chunk_l, chunk_r, far_sem, exc_sem, tile_sem, tile2_sem,
):
    r, c = lax.axis_index("row"), lax.axis_index("col")
    z, xl = r // 2, lax.rem(r, 2)
    y, xh, core = c // 4, lax.rem(c // 2, 2), lax.rem(c, 2)

    def col_of(dy, flip_x, flip_core=False):
        return (lax.rem(y + dy, 4) * 2 + (1 - xh if flip_x else xh)) * 2 + (1 - core if flip_core else core)

    def row_of(dz, flip_x):
        return lax.rem(z + dz, 4) * 2 + (1 - xl if flip_x else xl)

    partner = {"row": r, "col": col_of(0, False, True)}
    used = []
    numbers = iter(range(SENDS))

    def send(src, dst, recv_sem, device):
        copy = pltpu.make_async_remote_copy(
            src_ref=src, dst_ref=dst, send_sem=send_sem.at[next(numbers)], recv_sem=recv_sem,
            device_id=device, device_id_type=MESH,
        )
        copy.start()
        used.append(copy)

    def arrived(ref, recv_sem):
        pltpu.make_async_remote_copy(
            src_ref=ref, dst_ref=ref, send_sem=send_sem.at[0], recv_sem=recv_sem,
            device_id=partner, device_id_type=MESH,
        ).wait_recv()

    loads = [pltpu.make_async_copy(left, lv, local_sem.at[0])]
    for j in range(10):
        loads.append(pltpu.make_async_copy(
            right.at[:, pl.ds(j * BLK, BLK)], rv.at[pl.ds(j * 2 * BLK, 2 * BLK), :], local_sem.at[1 + j]))
    for load in loads:
        load.start()

    barrier = pltpu.get_barrier_semaphore()
    for d in range(1, 16):
        pl.semaphore_signal(barrier, inc=1, device_id={"row": r, "col": lax.rem(c + d, 16)}, device_id_type=MESH)
    for d in range(1, 8):
        pl.semaphore_signal(barrier, inc=1, device_id={"row": lax.rem(r + d, 8), "col": c}, device_id_type=MESH)

    def positions(mask_at, nxt):
        nxt[21] = jnp.int32(20)
        nxt[20] = jnp.int32(20)
        following = jnp.int32(20)
        count = jnp.int32(0)
        for b in reversed(range(20)):
            stored = mask_at(b) != 0
            following = jnp.where(stored, jnp.int32(b), following)
            nxt[b] = following
            count = count + jnp.where(stored, 1, 0)
        at = nxt[0]
        found = [at]
        for _ in range(S - 1):
            at = nxt[at + 1]
            found.append(at)
        return found, count

    pos_l, n_l = positions(lambda b: mask_l[b], next_l)
    pos_r, n_r = positions(lambda b: mask_r[b % 2, b // 2], next_r)
    weights = jnp.exp(-1.5 * gap[...])

    def own_l(t):
        return lv[pl.ds(jnp.minimum(pos_l[t], 19) * BLK, BLK), :] * weights

    def own_r(t):
        return rv[pl.ds(jnp.minimum(pos_r[t], 19) * BLK, BLK), :]

    for load in loads:
        load.wait()
    def pack(first, last):
        for t in range(first, last):
            out_l[t] = own_l(t)
            out_r[t] = own_r(t)

    NP = len(PIECES)
    ready = sum(1 for at, size in PIECES if at + size <= C - E)
    pieces = [pl.ds(at, size) for at, size in PIECES]
    ends = [at + size for at, size in PIECES]
    pack(0, ends[0])
    pl.semaphore_wait(barrier, 22)

    up_l, down_l, over_l = ({"row": r, "col": col_of(d, f)} for d, f in ((1, False), (3, False), (0, True)))
    up_r, down_r, over_r = ({"row": row_of(d, f), "col": c} for d, f in ((1, False), (3, False), (0, True)))

    def pass_l(chip_col, h, to, src=None):
        part = all_l.at[chip_col, pieces[h]]
        for device in to:
            send(part if src is None else src, part, chunk_l.at[chip_col, h], device)

    def pass_r(at_row, h, to, src=None):
        part = all_r.at[at_row, pieces[h]]
        for device in to:
            send(part if src is None else src, part, chunk_r.at[at_row, h], device)

    def pass_far(at_row, src=None):
        send(all_r.at[at_row, pl.ds(C - E, E)] if src is None else src, far_r.at[at_row], far_sem.at[at_row], partner)

    def split(block, at, slot):
        high = block.astype(jnp.bfloat16)
        at[slot, :, 0:BLK] = high
        at[slot, :, BLK:] = (block - high.astype(jnp.float32)).astype(jnp.bfloat16)

    def split_piece_l(chip_col, h, src):
        mate = chip_col + 1 - 2 * lax.rem(chip_col, 2)
        first, size = PIECES[h]

        def one(t, _):
            split(src[t], split_l, chip_col * S + t)
            return 0

        lax.fori_loop(first, first + size, one, 0)
        if first >= C - E:
            def other(t, _):
                split(src[t], split_l, mate * S + 2 * C - 1 - t)
                return 0

            lax.fori_loop(first, first + size, other, 0)

    def split_piece_r(at_row, h, src):
        first, size = PIECES[h]

        def one(t, _):
            split(src[t], split_r, at_row * S + t)
            return 0

        lax.fori_loop(first, first + size, one, 0)

    def keep_l(chip_col, h):
        split_piece_l(chip_col, h, all_l.at[chip_col])

    def keep_r(at_row, h):
        split_piece_r(at_row, h, all_r.at[at_row])

    def await_l(chip_col, h):
        arrived(all_l.at[chip_col, pieces[h]], chunk_l.at[chip_col, h])

    def await_r(at_row, h):
        arrived(all_r.at[at_row, pieces[h]], chunk_r.at[at_row, h])

    def from_partner(d, flip, h):
        chip_col = col_of(d, flip, True)
        await_l(chip_col, h)
        keep_l(chip_col, h)

    def far_blocks(d, flip):
        at_row = row_of(d, flip)
        arrived(far_r.at[at_row], far_sem.at[at_row])

        def one(q, _):
            split(far_r[at_row, q], split_r, at_row * S + S - 1 - q)
            return 0

        lax.fori_loop(0, E, one, 0)

    crossing = {}

    def own_piece(h):
        if h < AHEAD:
            cross(h)
        pass_l(c, h, (up_l, down_l), out_l.at[pieces[h]])
        pass_r(r, h, (up_r, down_r), out_r.at[pieces[h]])
        pass_l(c, h, (partner,), out_l.at[pieces[h]])

    def cross(h):
        pass_l(c, h, (over_l,), out_l.at[pieces[h]])
        pass_r(r, h, (over_r,), out_r.at[pieces[h]])
        crossing[h] = used[-2:]

    def cross_after(h):
        for copy in crossing[h - AHEAD]:
            copy.wait_send()
        used[:] = [copy for copy in used if all(copy is not done for done in crossing[h - AHEAD])]
        cross(h)

    own_piece(0)
    for q in range(E):
        exc_l[q] = own_l(C + q)
        exc_r[q] = own_r(C + q)
    send(exc_l, got_l, exc_sem.at[0], partner)
    send(exc_r, got_r, exc_sem.at[1], partner)
    for h in range(1, ready):
        pack(ends[h - 1], ends[h])
        own_piece(h)

    row_at = lax.broadcasted_iota(jnp.int32, (8, BLK), 0)
    lane_at = lax.broadcasted_iota(jnp.int32, (8, BLK), 1)
    note = jnp.where(lane_at == COUNT, jnp.where(row_at == 0, n_l, n_r), 20)
    for t in range(S):
        note = jnp.where(lane_at == t, jnp.where(row_at == 0, pos_l[t], pos_r[t]), note)
    tile[...] = note
    tiles[c] = note
    for d in range(1, 16):
        send(tile, tiles.at[c], tile_sem.at[c], {"row": r, "col": lax.rem(c + d, 16)})

    arrived(got_l, exc_sem.at[0])
    arrived(got_r, exc_sem.at[1])
    pack(ends[ready - 1], C - E)
    for t in range(C - E, C):
        out_l[t] = jnp.where(t < n_l, own_l(t), got_l[C - 1 - t])
        out_r[t] = jnp.where(t < n_r, own_r(t), got_r[C - 1 - t])
    for h in range(ready, NP):
        own_piece(h)
    pass_far(r, out_r.at[pl.ds(C - E, E)])
    def keep_own():
        for h in range(NP):
            split_piece_l(c, h, out_l)
            split_piece_r(r, h, out_r)

    def lists_l():
        for d in range(1, 16):
            other = lax.rem(c + d, 16)
            arrived(tiles.at[other], tile_sem.at[other])
        over = jnp.zeros((8, BLK), jnp.int32)
        for pair in range(8):
            one, two = tiles[2 * pair], tiles[2 * pair + 1]
            meta_l[pl.ds(2 * pair, 1), :] = one[0:1]
            meta_l[pl.ds(2 * pair + 1, 1), :] = two[0:1]
            full = jnp.where((one > C + E) | (two > C + E) | (one + two > 2 * C), 1, 0)
            over = jnp.maximum(over, full)
        over = jnp.where(lane_at == COUNT, over, 0)
        over = jnp.maximum(over[0:1], over[1:2])
        note2 = jnp.where(row_at == 0, note[1:2], over)
        tile2[...] = note2
        tiles2[r] = note2
        for d in range(1, 8):
            send(tile2, tiles2.at[r], tile2_sem.at[r], {"row": lax.rem(r + d, 8), "col": c})

    def lists_r():
        for d in range(1, 8):
            other = lax.rem(r + d, 8)
            arrived(tiles2.at[other], tile2_sem.at[other])
        flag = jnp.zeros((1, BLK), jnp.int32)
        for k in range(8):
            got = tiles2[k]
            meta_r[pl.ds(k, 1), :] = got[0:1]
            flag = jnp.maximum(flag, got[1:2])
        flag_out[...] = jnp.broadcast_to(flag, (8, BLK))

    def from_x(h):
        mine_l, mine_r = col_of(0, True), row_of(0, True)
        await_r(mine_r, h)
        pass_r(mine_r, h, (up_r, down_r))
        await_l(mine_l, h)
        pass_l(mine_l, h, (up_l, down_l, partner))
        if h == NP - 1:
            pass_far(mine_r)
        keep_r(mine_r, h)
        keep_l(mine_l, h)

    def from_ring(flip, h):
        for d in (3, 1):
            onward = (h in UP) == (d == 3)
            await_l(col_of(d, flip), h)
            pass_l(col_of(d, flip), h, (((up_l if d == 3 else down_l),) if onward else ()) + (partner,))
            await_r(row_of(d, flip), h)
            pass_r(row_of(d, flip), h, ((up_r if d == 3 else down_r),) if onward else ())
            if h == NP - 1:
                pass_far(row_of(d, flip))
        for d in (3, 1):
            keep_l(col_of(d, flip), h)
            keep_r(row_of(d, flip), h)

    def from_far(flip, h):
        await_l(col_of(2, flip), h)
        pass_l(col_of(2, flip), h, (partner,))
        await_r(row_of(2, flip), h)
        if h == NP - 1:
            pass_far(row_of(2, flip))
        keep_l(col_of(2, flip), h)
        keep_r(row_of(2, flip), h)

    events = [(0.12, keep_own, ()), (0.3, lists_l, ()), (1.1, lists_r, ())]
    for h in range(NP):
        share = ends[h] / C
        if h >= AHEAD:
            events.append((2 * ends[h - AHEAD] / C - 0.02, cross_after, (h,)))
        ring, x, far = share, 2 * share, 1 + share
        ring2, far2 = max(1.5, 2 * share) + share / 2 + 0.45, 3 + share
        events.append((ring, from_ring, (False, h)))
        events.append((x, from_x, (h,)))
        events.append((far, from_far, (False, h)))
        events.append((ring2, from_ring, (True, h)))
        events.append((far2, from_far, (True, h)))
        events.append((0.26 + share / 2, from_partner, (0, False, h)))
        for d in (1, 3):
            events.append((ring + 0.3, from_partner, (d, False, h)))
            events.append((ring2 + 0.3, from_partner, (d, True, h)))
        events.append((x + 0.3, from_partner, (0, True, h)))
        events.append((far + 0.3, from_partner, (2, False, h)))
        events.append((far2 + 0.3, from_partner, (2, True, h)))
    for d in range(4):
        for flip in (False, True):
            events.append(((1 if d == 0 else 2) + 1.1 + flip * 0.9 + 0.3 * d, far_blocks, (d, flip)))
    for _, what, how in sorted(events, key=lambda event: event[0]):
        what(*how)
    for copy in used:
        copy.wait_send()


SENDS = 136


def gather(left_factor, right_factor, pair_gap, mask_left, mask_right):
    smem = pl.BlockSpec(memory_space=pltpu.SMEM)
    vmem = pl.BlockSpec(memory_space=pltpu.VMEM)
    hbm = pl.BlockSpec(memory_space=pl.ANY)
    f32, i32 = jnp.float32, jnp.int32
    dma = pltpu.SemaphoreType.DMA
    return pl.pallas_call(
        gather_kernel,
        out_shape=(
            jax.ShapeDtypeStruct((16 * S + M_STEP, BLK, 2 * BLK), jnp.bfloat16),
            jax.ShapeDtypeStruct((8 * S, BLK, 2 * BLK), jnp.bfloat16),
            jax.ShapeDtypeStruct((16, BLK), i32),
            jax.ShapeDtypeStruct((8, BLK), i32),
            jax.ShapeDtypeStruct((8, BLK), i32),
        ),
        in_specs=[smem, smem, vmem, hbm, hbm],
        out_specs=(vmem,) * 5,
        scratch_shapes=[
            pltpu.VMEM((16, C, BLK, BLK), f32), pltpu.VMEM((8, C, BLK, BLK), f32), pltpu.VMEM((8, E, BLK, BLK), f32),
            pltpu.VMEM((20 * BLK, BLK), f32), pltpu.VMEM((20 * BLK, BLK), f32),
            pltpu.SMEM((22,), i32), pltpu.SMEM((22,), i32),
            pltpu.VMEM((C, BLK, BLK), f32), pltpu.VMEM((C, BLK, BLK), f32),
            pltpu.VMEM((E, BLK, BLK), f32), pltpu.VMEM((E, BLK, BLK), f32),
            pltpu.VMEM((E, BLK, BLK), f32), pltpu.VMEM((E, BLK, BLK), f32),
            pltpu.VMEM((8, BLK), i32), pltpu.VMEM((16, 8, BLK), i32),
            pltpu.VMEM((8, BLK), i32), pltpu.VMEM((8, 8, BLK), i32),
            dma((13,)), dma((SENDS,)), dma((16, len(PIECES))), dma((8, len(PIECES))), dma((8,)), dma((2,)), dma((16,)), dma((8,)),
        ],
        compiler_params=pltpu.CompilerParams(
            collective_id=0, has_side_effects=True, vmem_limit_bytes=30 << 20),
    )(mask_left.reshape(20), mask_right, pair_gap.reshape(1, BLK), left_factor, right_factor)


CUTS = (8, 12, 14, 15, 16)
W = 12
ENTRIES = 16 * 5 * 5 + 2


def product_kernel(meta_l, meta_r, split_l, split_r, update, acc, slot_of, strip_of, left_of, right_of, steps_of, last_of, sem_o):
    def count(meta, at):
        return jnp.minimum(meta[at, COUNT], S)

    def zero(i, _):
        rows = pl.ds(pl.multiple_of(lax.rem(i, 10) * 256, 256), 256)
        acc[i // 10, rows, :] = jnp.zeros((256, BLK), jnp.float32)
        for n in (2 * i, 2 * i + 1):
            slot_of[n] = jnp.int32(0)
            strip_of[n] = jnp.int32(10)
        return 0

    lax.fori_loop(0, 17 * W // 2, zero, 0)
    for j in range(10):
        last_of[j] = jnp.int32(-1)

    def sort_r(k, total):
        def one(t, ends):
            b = meta_r[k, t]
            odd = lax.rem(b, 2)
            place = (2 * k + odd) * W + jnp.where(odd == 1, ends[1], ends[0])
            slot_of[place] = k * S + t
            strip_of[place] = b // 2
            last_of[b // 2] = 2 * k + odd
            return ends[0] + 1 - odd, ends[1] + odd

        ends = lax.fori_loop(0, count(meta_r, k), one, (jnp.int32(0), jnp.int32(0)))
        for odd in range(2):
            pair = 2 * k + odd
            steps = (count(meta_l, pair) + M_STEP - 1) // M_STEP

            def across(q, total):
                def down(u, total):
                    left_of[total] = pair * 4 + u
                    right_of[total] = pair * W + 2 * q
                    return total + 1

                return lax.fori_loop(0, steps, down, total)

            total = lax.fori_loop(0, (ends[odd] + 1) // 2, across, total)
            steps_of[pair] = total
        return total

    total = lax.fori_loop(0, 8, sort_r, jnp.int32(0))
    left_of[total] = jnp.int32(0)
    right_of[total] = jnp.int32(16 * W)

    def step(n):
        at_l, at_r = left_of[n], right_of[n]
        k, u = at_l // 4, lax.rem(at_l, 4)
        one, two = split_r[slot_of[at_r]], split_r[slot_of[at_r + 1]]
        highs = jnp.concatenate([one[:, :BLK], two[:, :BLK]], axis=1)
        lows = jnp.concatenate([one[:, BLK:], two[:, BLK:]], axis=1)
        weights = jnp.concatenate([highs, highs, lows], axis=0)
        lhs = split_l[pl.ds(k * S + u * M_STEP, M_STEP)].reshape(M_STEP * BLK, 2 * BLK)
        lhs = jnp.concatenate([lhs, lhs[:, :BLK]], axis=1)
        return k, u, at_r, jnp.dot(lhs, weights, preferred_element_type=jnp.float32)

    def store(k, u, at_r, full):
        for v in range(M_STEP):
            rows = pl.ds(pl.multiple_of(meta_l[k, u * M_STEP + v] * BLK, BLK), BLK)
            for w in range(2):
                acc[strip_of[at_r + w], rows, :] += full[v * BLK:(v + 1) * BLK, w * BLK:(w + 1) * BLK]

    def two_steps(n, _):
        first = step(2 * n)
        second = step(2 * n + 1)
        store(*first)
        store(*second)
        return 0

    outs = [
        pltpu.make_async_copy(acc.at[j, pl.ds(0, 20 * BLK)], update.at[:, pl.ds(j * BLK, BLK)], sem_o.at[j])
        for j in range(10)
    ]
    done, before = jnp.int32(0), -1
    for pairs in CUTS:
        now = (steps_of[pairs - 1] + 1) // 2
        lax.fori_loop(done, now, two_steps, 0)
        for j in range(10):
            last = last_of[j]

            @pl.when((last >= before) & (last < pairs))
            def _():
                outs[j].start()

        done, before = now, pairs
    for copy in outs:
        copy.wait()


def product(meta_l, meta_r, split_l, split_r):
    smem = pl.BlockSpec(memory_space=pltpu.SMEM)
    vmem = pl.BlockSpec(memory_space=pltpu.VMEM)
    f32, i32 = jnp.float32, jnp.int32
    return pl.pallas_call(
        product_kernel,
        out_shape=jax.ShapeDtypeStruct((20 * BLK, 10 * BLK), f32),
        in_specs=[smem, smem, vmem, vmem],
        out_specs=pl.BlockSpec(memory_space=pl.ANY),
        scratch_shapes=[
            pltpu.VMEM((11, 21 * BLK, BLK), f32),
            pltpu.SMEM((17 * W,), i32), pltpu.SMEM((17 * W,), i32),
            pltpu.SMEM((ENTRIES,), i32), pltpu.SMEM((ENTRIES,), i32),
            pltpu.SMEM((16,), i32), pltpu.SMEM((10,), i32),
            pltpu.SemaphoreType.DMA((10,)),
        ],
        compiler_params=pltpu.CompilerParams(vmem_limit_bytes=24 << 20),
    )(meta_l, meta_r, split_l, split_r)


def per_device(left_factor, right_factor, pair_gap, mask_left, mask_right):
    split_l, split_r, meta_l, meta_r, flag = gather(left_factor, right_factor, pair_gap, mask_left, mask_right)
    return lax.cond(
        flag[0, COUNT] > 0,
        lambda: dense_path(left_factor, right_factor, pair_gap, mask_left, mask_right),
        lambda: product(meta_l, meta_r, split_l, split_r),
    )


def solution(mesh):
    return jax.shard_map(
        per_device,
        mesh=mesh,
        in_specs=(P("row", "col"), P("row", "col"), P("col"), P("row", "col"), P("row", "col")),
        out_specs=P("row", "col"),
        check_vma=False,
    )
```
